32 devices in a mesh: groups: 2 (over x), expert: 16 (over z, y, core).
Axes of the slice: x: 2, y: 2, z: 4, core: 2. Of those that a mesh axis runs over, the one named last changes fastest.
Arguments:
- hidden_in: bfloat16 [256, 6400], P(('groups', 'expert')), parts along dimension 0, may hold values from -6 to 6
- norm_gain: float32 [6400], replicated, may hold values from 0.1 to 1.9
- router: bfloat16 [6400, 2], replicated, may hold values from -0.078125 to 0.078125
- routes: int32 [256, 1], P(('groups', 'expert')), parts along dimension 0, may hold values from 0 to 1; in each aligned block of 8 rows (0 to 7, 8 to 15, ...) at most 6 rows name the same one
- routed_gate_up: bfloat16 [16, 6400, 576], P('expert'), may hold values from -0.078125 to 0.078125
- routed_down: bfloat16 [16, 288, 6400], P('expert'), may hold values from -0.125 to 0.125
Outputs:
- mixed: bfloat16 [256, 6400], P(('groups', 'expert')), parts along dimension 0
The draws below stay inside these ranges and needn't reach their ends.
There are 2 independent parts, one for each index of `groups`. The reference program is written for one: setup_inputs(seed, part) draws one part's arguments, and reference() takes and returns one part's arrays. A program takes and returns all parts, laid end to end along the dimension named above; an argument that names none is the same for every part. Nothing has to cross between parts.
Inputs may be any that keep to these rules, and one draw needn't show every extreme that they name: `routes`: among the rows of one device no expert is named by more than 6 rows, and in every draw some device names one expert exactly 6 times.
All inputs are finite; a program needn't handle non-finite values.
Results may differ from the reference program's by a relative error of at most 0.0049.
Values may be sent and summed in bfloat16 or wider, within the bound.
No kernel may reach another device: no remote copies, remote signals or barrier semaphores. Data moves between devices by JAX's collectives and lax.ppermute only.
A program may use at most 128 MiB of HBM per device.

```python
import math
import jax
import jax.numpy as jnp
import numpy as np
from jax import lax

D = 6400
EXPERTS = 2
FF_DEV = 288
TOK_DEV = 8
CAP = 6
TOKENS = 128
SPLIT = 8
N_EXPERT = 16


def block_levels(rng, dims, split, least, top_value):
    def one(axis_at, blocks):
        steps = jax.random.uniform(jax.random.fold_in(jax.random.fold_in(rng, 6), axis_at), (blocks,), jnp.float32, least / len(split), top_value / len(split))
        return jnp.repeat(jnp.exp(steps), dims[axis_at] // blocks).reshape((-1,) + (1,) * (len(dims) - axis_at - 1))

    factor_of = one(*split[0])
    for cut in split[1:]:
        factor_of = factor_of * one(*cut)
    return factor_of


def routed_block(stream_key, own, number, rows, amount, top, bound, lean):
    order = jax.random.permutation(stream_key, amount)
    packed, usual = portions_of(amount, rows * top, bound, lean, True), portions_of(amount, rows * top, bound, lean, False)
    places = jnp.arange(amount)

    def named(sizes, rotation):
        used = int((sizes > 0).sum())
        fixed = max(1, used // 4)
        shifted = fixed + (places - fixed + rotation * (used - fixed)) % max(1, amount - fixed)
        return jnp.zeros((amount,), jnp.int32).at[order[jnp.where(places < fixed, places, shifted)]].set(jnp.asarray(sizes, jnp.int32))

    sizes = jnp.where(number % 4 == 0, named(packed, number // 4), named(usual, number - number // 4 - 1))
    mixed = jax.random.permutation(jax.random.fold_in(own, 3), amount)
    giver, receiver = mixed[0:amount // 2 * 2:2], mixed[1:amount // 2 * 2:2]
    margin = jnp.minimum(sizes[giver] - 1, bound - sizes[receiver]) // 2
    margin = jnp.where((giver == order[0]) | (receiver == order[0]) | (sizes[receiver] == 0), 0, jnp.maximum(margin, 0))
    shifted = jax.random.randint(jax.random.fold_in(own, 4), (amount // 2,), 0, 1 << 20) % (margin + 1)
    sizes = sizes.at[giver].add(-shifted).at[receiver].add(shifted)
    members = jnp.searchsorted(jnp.cumsum(sizes), jnp.arange(rows * top), side="right").astype(jnp.int32)
    grid = members.reshape(top, rows).T
    grid = grid[jax.random.permutation(jax.random.fold_in(own, 1), rows)]
    rotation = jax.random.randint(jax.random.fold_in(own, 2), (rows, 1), 0, top)
    return jnp.take_along_axis(grid, (jnp.arange(top)[None, :] + rotation) % top, axis=1)


def portions_of(count, total, limit, lean, full):
    weights = [(1 << 20) // math.isqrt(rank ** lean) + 1 for rank in range(1, count + 1)]
    largest = limit if full else min(limit, max(-(-total // count), total * weights[0] // sum(weights)))
    least = 1 if total - largest >= count - 1 else 0
    given, surplus = [largest] + [least] * (count - 1), total - largest - least * (count - 1)
    while surplus > 0:
        candidates = [i for i in range(1, count) if given[i] < largest] or [i for i in range(1, count) if given[i] < limit]
        whole, left = sum([weights[i] for i in candidates]), surplus
        for i in candidates:
            extra = min(limit - given[i], max(1, left * weights[i] // whole), surplus)
            given[i] = given[i] + extra
            surplus = surplus - extra
    return np.array(given)


def centred(own_key, extent, spread, limit, shards=(), kind=jnp.bfloat16):
    values = spread * jax.random.normal(own_key, extent, jnp.float32)
    if shards:
        values = values * block_levels(own_key, extent, shards, -0.22, 0.18)
    return jnp.clip(values, -limit, limit).astype(kind)


def setup_inputs(seed: int = 0, part: int = 0) -> dict:
    splits = jax.random.split(jax.random.key(seed), 7)
    own_keys = jax.random.split(jax.random.fold_in(splits[6], part), 7)
    hidden_in = centred(own_keys[0], (TOKENS, D), 1.0, 6.0, ((0, 16),))
    norm_gain = jnp.clip(1.0 + 0.18 * jax.random.normal(splits[1], (D,), jnp.float32), 0.1, 1.9)
    router = centred(splits[2], (D, EXPERTS), D ** -0.5, 0.078125)
    routes_keys = jax.random.split(jax.random.fold_in(own_keys[3], 1), TOKENS // TOK_DEV)
    routes_turns = jax.random.permutation(jax.random.fold_in(own_keys[3], 3), TOKENS // TOK_DEV)
    routes = jax.vmap(lambda own, number: routed_block(jax.random.fold_in(own_keys[3], 2), own, number, TOK_DEV, EXPERTS, 1, CAP, 2))(routes_keys, routes_turns).reshape((TOKENS, 1))
    routed_gate_up = centred(splits[4], (N_EXPERT, D, 2 * FF_DEV), D ** -0.5, 0.078125, ((0, 16),))
    routed_down = centred(splits[5], (N_EXPERT, FF_DEV, D), (FF_DEV * SPLIT) ** -0.5, 0.125, ((0, 16),))
    return {"hidden_in": hidden_in, "norm_gain": norm_gain, "router": router, "routes": routes, "routed_gate_up": routed_gate_up, "routed_down": routed_down}


def rms_norm(hidden_in, norm_gain):
    values = hidden_in.astype(jnp.float32)
    mean_square = lax.optimization_barrier(jnp.mean(values * values, axis=-1, keepdims=True))
    return (values * lax.rsqrt(mean_square + 1e-06) * norm_gain.astype(jnp.float32)).astype(jnp.bfloat16)

def reference(hidden_in, norm_gain, router, routes, routed_gate_up, routed_down):
    normed = rms_norm(hidden_in, norm_gain)
    logits = jnp.dot(normed, router, preferred_element_type=jnp.float32)
    scores = jax.nn.sigmoid(jnp.take_along_axis(logits, routes, axis=1))
    copies = N_EXPERT // EXPERTS
    hidden_units = routed_down.shape[1]

    def accumulate(carry_sum, inputs):
        gate_up, down_w, slice_id = inputs
        lifted = jnp.dot(normed, gate_up, preferred_element_type=jnp.float32)
        act = (jax.nn.silu(lifted[:, :hidden_units]) * lifted[:, hidden_units:]).astype(jnp.bfloat16)
        output = jnp.dot(act, down_w, preferred_element_type=jnp.float32)
        chosen = routes == slice_id // copies
        return (carry_sum + jnp.where(chosen, output * scores, jnp.zeros_like(output)), None)
    start_sum = jnp.zeros((hidden_in.shape[0], hidden_in.shape[1]), jnp.float32)
    routed, _ = lax.scan(accumulate, start_sum, (routed_gate_up, routed_down, jnp.arange(N_EXPERT, dtype=jnp.int32)))
    return (hidden_in.astype(jnp.float32) + routed).astype(jnp.bfloat16)
```

```python
import jax
import jax.numpy as jnp
from jax import lax
from jax.sharding import PartitionSpec as P


def rms_norm(hidden_in, norm_gain):
    values = hidden_in.astype(jnp.float32)
    mean_square = jnp.mean(values * values, axis=-1, keepdims=True)
    return (values * lax.rsqrt(mean_square + 1e-06) * norm_gain).astype(jnp.bfloat16)


def expert_rows(rows, norm_gain, gate_up, down_w, column):
    normed = rms_norm(rows, norm_gain)
    hidden_units = down_w.shape[0]
    lifted = jnp.dot(normed, gate_up, preferred_element_type=jnp.float32)
    act = (jax.nn.silu(lifted[:, :hidden_units]) * lifted[:, hidden_units:]).astype(jnp.bfloat16)
    output = jnp.dot(act, down_w, preferred_element_type=jnp.float32)
    scores = jax.nn.sigmoid(jnp.dot(normed, column, preferred_element_type=jnp.float32))
    return output * scores


def steps_of(axis_len, copies):
    masks = []
    mask = 2
    while mask < copies:
        masks.append(mask)
        mask *= 2
    steps = []
    for first, second in zip(masks, masks[::-1]):
        steps.append([(i, i ^ (second if i % 2 else first)) for i in range(axis_len)])
    return steps


def flip(axis_len, mask):
    return [(i, i ^ mask) for i in range(axis_len)]


def body(hidden_in, norm_gain, router, routes, routed_gate_up, routed_down):
    axis_len = lax.axis_size("expert")
    experts = router.shape[1]
    copies = axis_len // experts
    own_expert = lax.axis_index("expert") // copies
    column = lax.dynamic_slice_in_dim(router, own_expert, 1, 1)
    steps = steps_of(axis_len, copies)

    def swap(block, pairs):
        return lax.ppermute(block, "expert", pairs)

    blocks = hidden_in[None]
    mask = copies
    while mask < axis_len:
        blocks = jnp.concatenate([blocks, swap(blocks, flip(axis_len, mask))], axis=0)
        mask *= 2
    for pairs in steps:
        blocks = jnp.concatenate([blocks, swap(blocks, pairs)], axis=0)
    blocks = jnp.concatenate([blocks, swap(blocks, flip(axis_len, 1))], axis=0)
    rows = blocks.reshape(-1, blocks.shape[-1])
    result = expert_rows(rows, norm_gain, routed_gate_up[0], routed_down[0], column)
    part = result.reshape(blocks.shape)

    def fold(part, pairs):
        half = part.shape[0] // 2
        arrived = swap(part[half:].astype(jnp.bfloat16), pairs)
        return part[:half] + arrived.astype(jnp.float32)

    part = fold(part, flip(axis_len, 1))
    for pairs in steps[::-1]:
        part = fold(part, pairs)
    chosen = part[0]
    for k in range(1, experts):
        arrived = swap(part[k].astype(jnp.bfloat16), flip(axis_len, copies * k))
        other = jnp.bitwise_xor(own_expert, k)
        chosen = jnp.where(routes == other, arrived.astype(jnp.float32), chosen)
    return (hidden_in.astype(jnp.float32) + chosen).astype(jnp.bfloat16)


def solution(mesh):
    placed = (
        P(("groups", "expert"), None),
        P(),
        P(),
        P(("groups", "expert"), None),
        P("expert", None, None),
        P("expert", None, None),
    )
    return jax.shard_map(
        body, mesh=mesh, in_specs=placed, out_specs=P(("groups", "expert"), None), check_vma=False
    )
```

```python
import functools

import jax
import jax.numpy as jnp
from jax import lax
from jax.experimental import pallas as pl
from jax.experimental.pallas import tpu as pltpu
from jax.sharding import PartitionSpec as P


def pick_chunk(width, most):
    chunk = most
    while width % chunk:
        chunk -= 128
    return chunk


def expert_kernel(copies, count, *refs):
    block_refs, refs = refs[:count], refs[count:]
    gain_ref, router_ref, up_ref, down_ref = refs[:4]
    out_refs, normed_ref = refs[4 : 4 + count], refs[4 + count]
    tok_rows, width = block_refs[0].shape
    units = down_ref.shape[0]
    chunk = pick_chunk(width, 1280)
    for first in range(0, count, 2):
        pair = block_refs[first : first + 2]

        def load(at):
            return jnp.concatenate([ref[:, at : at + chunk].astype(jnp.float32) for ref in pair], axis=0)

        total = jnp.zeros((2 * tok_rows, chunk), jnp.float32)
        for at in range(0, width, chunk):
            values = load(at)
            total = total + values * values
        mean_square = jnp.sum(total, axis=1, keepdims=True) * (1.0 / width)
        factor = lax.rsqrt(mean_square + 1e-06)
        for at in range(0, width, chunk):
            normed = load(at) * factor * gain_ref[:, at : at + chunk]
            normed_ref[first * tok_rows : (first + 2) * tok_rows, at : at + chunk] = normed.astype(jnp.bfloat16)
    nt = (((1,), (1,)), ((), ()))
    normed = normed_ref[...]
    lifted = lax.dot_general(normed, up_ref[...], nt, preferred_element_type=jnp.float32)
    gate, up = lifted[:, :units], lifted[:, units:]
    act = (gate / (1.0 + jnp.exp(-gate)) * up).astype(jnp.bfloat16)
    logits = lax.dot_general(normed, router_ref[...], nt, preferred_element_type=jnp.float32)
    own = lax.axis_index("expert") // copies
    columns = lax.broadcasted_iota(jnp.int32, logits.shape, 1)
    logit = jnp.sum(jnp.where(columns == own, logits, 0.0), axis=1, keepdims=True)
    scores = 1.0 / (1.0 + jnp.exp(-logit))
    for at in range(0, width, chunk):
        output = jnp.dot(act, down_ref[:, at : at + chunk], preferred_element_type=jnp.float32) * scores
        for k in range(count):
            out_refs[k][:, at : at + chunk] = output[k * tok_rows : (k + 1) * tok_rows].astype(jnp.bfloat16)


def expert_rows(blocks, norm_gain, router, gate_up, down_w, copies):
    count = len(blocks)
    tok_rows, width = blocks[0].shape
    units = down_w.shape[0]
    rows = count * tok_rows
    vmem = pl.BlockSpec(memory_space=pltpu.VMEM)
    gate_up = pltpu.with_memory_space_constraint(gate_up, pltpu.VMEM)
    down_w = pltpu.with_memory_space_constraint(down_w, pltpu.VMEM)
    return pl.pallas_call(
        functools.partial(expert_kernel, copies, count),
        out_shape=[jax.ShapeDtypeStruct((tok_rows, width), jnp.bfloat16)] * count,
        in_specs=[vmem] * (count + 4),
        out_specs=[vmem] * count,
        scratch_shapes=[pltpu.VMEM((rows, width), jnp.bfloat16)],
        compiler_params=pltpu.CompilerParams(vmem_limit_bytes=40 * 1024 * 1024),
        cost_estimate=pl.CostEstimate(
            flops=6 * rows * width * units,
            bytes_accessed=6 * units * width,
            transcendentals=rows * units,
        ),
    )(*blocks, norm_gain[None, :], router.T, gate_up, down_w)


def body(hidden_in, norm_gain, router, routes, routed_gate_up, routed_down):
    axis_len = lax.axis_size("expert")
    experts = router.shape[1]
    copies = axis_len // experts
    own_expert = lax.axis_index("expert") // copies
    chips = list(range(2, copies, 2))[::-1]

    def swap(block, mask):
        return lax.ppermute(block, "expert", [(i, i ^ mask) for i in range(axis_len)])

    far = [swap(hidden_in, copies * k) for k in range(1, experts)]
    sources = [hidden_in] + far
    mine = [[block] + [swap(block, mask) for mask in chips] for block in sources]
    theirs = [[swap(block, 1) for block in group] for group in mine]
    flat = sum(mine, []) + sum(theirs, [])
    outs = expert_rows(flat, norm_gain, router, routed_gate_up[0].T, routed_down[0], copies)
    size = len(chips) + 1
    kept = [outs[k * size : (k + 1) * size] for k in range(experts)]
    given = [outs[(experts + k) * size : (experts + k + 1) * size] for k in range(experts)]

    def fold(own_parts, given_parts):
        back = [swap(part, 1) for part in given_parts]
        both = [a.astype(jnp.float32) + b.astype(jnp.float32) for a, b in zip(own_parts, back)]
        total = both[0]
        for part, mask in zip(both[1:], chips):
            total = total + swap(part.astype(jnp.bfloat16), mask).astype(jnp.float32)
        return total

    chosen = None
    for k in list(range(1, experts)) + [0]:
        total = fold(kept[k], given[k])
        if k:
            total = swap(total.astype(jnp.bfloat16), copies * k).astype(jnp.float32)
        other = jnp.bitwise_xor(own_expert, k)
        chosen = total if chosen is None else jnp.where(routes == other, total, chosen)
    return (hidden_in.astype(jnp.float32) + chosen).astype(jnp.bfloat16)


def solution(mesh):
    placed = (
        P(("groups", "expert"), None),
        P(),
        P(),
        P(("groups", "expert"), None),
        P("expert", None, None),
        P("expert", None, None),
    )
    return jax.shard_map(
        body, mesh=mesh, in_specs=placed, out_specs=P(("groups", "expert"), None), check_vma=False
    )
```

```python
import functools

import jax
import jax.numpy as jnp
from jax import lax
from jax.experimental import pallas as pl
from jax.experimental.pallas import tpu as pltpu
from jax.sharding import PartitionSpec as P


def pick_chunk(width, most):
    chunk = most
    while width % chunk:
        chunk -= 128
    return chunk


def fetch_kernel(count, *refs):
    sources, targets, sems = refs[:count], refs[count + 1 : -1], refs[-1]
    moves = [pltpu.make_async_copy(a, b, sems.at[k]) for k, (a, b) in enumerate(zip(sources, targets))]
    for move in moves:
        move.start()
    for move in moves:
        move.wait()


def fetched(arrays, after):
    count = len(arrays)
    arrays = [pltpu.with_memory_space_constraint(x, pltpu.HBM) for x in arrays]
    size = sum(x.size * x.dtype.itemsize for x in arrays)
    return pl.pallas_call(
        functools.partial(fetch_kernel, count),
        out_shape=[jax.ShapeDtypeStruct(x.shape, x.dtype) for x in arrays],
        in_specs=[pl.BlockSpec(memory_space=pltpu.HBM)] * count + [pl.BlockSpec(memory_space=pl.ANY)],
        out_specs=[pl.BlockSpec(memory_space=pl.ANY)] * count,
        scratch_shapes=[pltpu.SemaphoreType.DMA((count,))],
        compiler_params=pltpu.CompilerParams(vmem_limit_bytes=1024 * 1024),
        cost_estimate=pl.CostEstimate(flops=0, bytes_accessed=size, transcendentals=0),
    )(*arrays, after)


def expert_kernel(copies, count, *refs):
    block_refs, refs = refs[:count], refs[count:]
    gain_ref, router_ref, up_ref, down_far = refs[:4]
    out_refs, (down_held, normed_ref, sems) = refs[4 : 4 + count], refs[4 + count :]
    tok_rows, width = block_refs[0].shape
    units = down_far.shape[0]
    chunk = pick_chunk(width, 1280)
    steps = range(0, width, chunk)
    piece = units // 3
    waits = []
    for k in range(3):
        window = pl.ds(k * piece, piece)
        waits.append(pltpu.make_async_copy(down_far.at[window], down_held.at[window], sems.at[k]))
        waits[-1].start()
    pairs = [(first, block_refs[first : first + 2]) for first in range(0, count, 2)]

    def load(pair, at):
        return jnp.concatenate([ref[:, at : at + chunk].astype(jnp.float32) for ref in pair], axis=0)

    factors = []
    for first, pair in pairs:
        total = jnp.zeros((2 * tok_rows, chunk), jnp.float32)
        for at in steps:
            values = load(pair, at)
            total = total + values * values
        mean_square = jnp.sum(total, axis=1, keepdims=True) * (1.0 / width)
        factors.append(lax.rsqrt(mean_square + 1e-06))
    nt = (((1,), (1,)), ((), ()))
    for at in steps:
        lines = [gain_ref[j : j + 1, :] for j in range(at // 128, (at + chunk) // 128)]
        gain = jnp.concatenate(lines, axis=1)
        for factor, (first, pair) in zip(factors, pairs):
            normed = load(pair, at) * factor * gain
            normed_ref[first * tok_rows : (first + 2) * tok_rows, at : at + chunk] = normed.astype(jnp.bfloat16)
    logits = lax.dot_general(normed_ref[...], router_ref[...], nt, preferred_element_type=jnp.float32)
    lifted = lax.dot_general(normed_ref[...], up_ref[...], nt, preferred_element_type=jnp.float32)
    own = lax.axis_index("expert") // copies
    columns = lax.broadcasted_iota(jnp.int32, logits.shape, 1)
    logit = jnp.sum(jnp.where(columns == own, logits, 0.0), axis=1, keepdims=True)
    scores = 1.0 / (1.0 + jnp.exp(-logit))
    gate, up = lifted[:, :units], lifted[:, units:]
    act = (gate / (1.0 + jnp.exp(-gate)) * up).astype(jnp.bfloat16)
    for move in waits:
        move.wait()
    for at in steps:
        output = jnp.dot(act, down_held[:, at : at + chunk], preferred_element_type=jnp.float32) * scores
        for k in range(count):
            out_refs[k][:, at : at + chunk] = output[k * tok_rows : (k + 1) * tok_rows].astype(jnp.bfloat16)


def expert_rows(blocks, norm_gain, router, gate_up, down_w, copies):
    count = len(blocks)
    tok_rows, width = blocks[0].shape
    units = down_w.shape[0]
    rows = count * tok_rows
    vmem = pl.BlockSpec(memory_space=pltpu.VMEM)
    return pl.pallas_call(
        functools.partial(expert_kernel, copies, count),
        out_shape=[jax.ShapeDtypeStruct((tok_rows, width), jnp.bfloat16)] * count,
        in_specs=[vmem] * (count + 3) + [pl.BlockSpec(memory_space=pltpu.HBM)],
        out_specs=[vmem] * count,
        scratch_shapes=[
            pltpu.VMEM(down_w.shape, jnp.bfloat16),
            pltpu.VMEM((rows, width), jnp.bfloat16),
            pltpu.SemaphoreType.DMA((3,)),
        ],
        compiler_params=pltpu.CompilerParams(vmem_limit_bytes=32 * 1024 * 1024),
        cost_estimate=pl.CostEstimate(
            flops=6 * rows * width * units,
            bytes_accessed=6 * units * width,
            transcendentals=rows * units,
        ),
    )(*blocks, norm_gain, router, gate_up, pltpu.with_memory_space_constraint(down_w, pltpu.HBM))


def body(hidden_in, norm_gain, router, routes, routed_gate_up, routed_down):
    axis_len = lax.axis_size("expert")
    experts = router.shape[1]
    copies = axis_len // experts
    own_expert = lax.axis_index("expert") // copies
    chips = list(range(2, copies, 2))[::-1]
    size = len(chips) + 1

    def swap(block, mask):
        return lax.ppermute(block, "expert", [(i, i ^ mask) for i in range(axis_len)])

    far = [swap(hidden_in, copies * k) for k in range(1, experts)]
    mine = [[source] + [swap(source, mask) for mask in chips] for source in [hidden_in] + far]
    local = [routed_gate_up[0].T, router.T, norm_gain.reshape(-1, 128), hidden_in]
    gate_up, router_t, gain, mine[0][0] = fetched(local, mine[0][-1])
    gate_up, mine[0][1:], mine[1:] = lax.optimization_barrier((gate_up, mine[0][1:], mine[1:]))
    theirs = [[swap(block, 1) for block in group] for group in [[hidden_in] + mine[0][1:]] + mine[1:]]
    outs = expert_rows(sum(mine, []) + sum(theirs, []), gain, router_t, gate_up, routed_down[0], copies)
    kept = [outs[k * size : (k + 1) * size] for k in range(experts)]
    given = [outs[(experts + k) * size : (experts + k + 1) * size] for k in range(experts)]

    def both_cores(own_parts, given_parts):
        back = [swap(part, 1) for part in given_parts]
        both = [a.astype(jnp.float32) + b.astype(jnp.float32) for a, b in zip(own_parts, back)]
        return both[:1] + [part.astype(jnp.bfloat16) for part in both[1:]]

    def fold(both):
        total = both[0]
        for part, mask in zip(both[1:], chips):
            total = total + swap(part, mask).astype(jnp.float32)
        return total

    sums = [fold(both_cores(kept[k], given[k])).astype(jnp.bfloat16) for k in range(1, experts)]
    near = both_cores(kept[0], given[0])
    sums, near[3:] = lax.optimization_barrier((sums, near[3:]))
    near = fold(near)
    chosen = near
    for k, total in enumerate(sums, start=1):
        arrived = swap(total, copies * k).astype(jnp.float32)
        chosen = jnp.where(routes == jnp.bitwise_xor(own_expert, k), arrived, chosen)
    return (hidden_in.astype(jnp.float32) + chosen).astype(jnp.bfloat16)


def solution(mesh):
    placed = (
        P(("groups", "expert"), None),
        P(),
        P(),
        P(("groups", "expert"), None),
        P("expert", None, None),
        P("expert", None, None),
    )
    return jax.shard_map(
        body, mesh=mesh, in_specs=placed, out_specs=P(("groups", "expert"), None), check_vma=False
    )
```

```python
import functools

import jax
import jax.numpy as jnp
from jax import lax
from jax.experimental import pallas as pl
from jax.experimental.pallas import tpu as pltpu
from jax.sharding import PartitionSpec as P


def fold_of(tok_rows, width):
    slots = max(2, 3 * tok_rows // 4)
    per = -(-slots // (tok_rows - slots))
    rest = width // (per + 1) // 128 * 128
    return slots, per, width - rest


def folded(main, rest, slots, per):
    spare = []
    for first in range(0, slots, per):
        lines = [rest[k : k + 1] for k in range(first, min(first + per, slots))]
        pad = main.shape[1] - len(lines) * rest.shape[1]
        spare.append(jnp.concatenate(lines + [jnp.zeros((1, pad), jnp.float32)], axis=1))
    return jnp.concatenate([main[:slots]] + spare, axis=0)


def unfolded(load, tok_rows, rest, slots, per):
    lines = []
    for k in range(slots):
        at = k % per * rest
        lines.append(load(at, rest)[slots + k // per : slots + k // per + 1])
    return jnp.concatenate(lines + [jnp.zeros((tok_rows - slots, rest), jnp.float32)], axis=0)


def places(routes_ref, tok_rows):
    shape = (tok_rows, tok_rows)
    row = jnp.broadcast_to(routes_ref[...], shape)
    down = lax.broadcasted_iota(jnp.int32, shape, 0)
    across = lax.broadcasted_iota(jnp.int32, shape, 1)
    column = jnp.sum(jnp.where(down == across, row, 0), axis=1, keepdims=True)
    same = column == row
    rank_row = jnp.sum(jnp.where(same & (down < across), 1, 0), axis=0, keepdims=True)
    rank_column = jnp.sum(jnp.where(same & (across < down), 1, 0), axis=1, keepdims=True)
    return row, column, rank_row, rank_column, down, across


def pack_kernel(copies, experts, routes_far, hidden_far, *refs):
    out_refs, (routes_ref, hidden_ref, packed_ref, sems) = refs[:experts], refs[experts:]
    moves = [(routes_far, routes_ref), (hidden_far, hidden_ref)]
    moves = [pltpu.make_async_copy(x, y, sems.at[k]) for k, (x, y) in enumerate(moves)]
    for move in moves:
        move.start()
    tok_rows, width = hidden_ref.shape
    slots, per, stay = fold_of(tok_rows, width)
    own = lax.axis_index("expert") // copies
    moves[0].wait()
    row, _, rank, _, down, _ = places(routes_ref, tok_rows)
    picks = []
    for k in range(experts):
        expert = jnp.bitwise_xor(own, k)
        picks.append(jnp.where((row == expert) & (rank == down) & (down < slots), 1.0, 0.0))
    pick = jnp.concatenate(picks, axis=0).astype(jnp.bfloat16)
    moves[1].wait()
    sorted_rows = jnp.dot(pick, hidden_ref[...], preferred_element_type=jnp.float32)
    lasts = []
    for k in range(experts)[::-1]:
        rows = sorted_rows[k * tok_rows : (k + 1) * tok_rows]
        packed_ref[k] = folded(rows[:, :stay], rows[:, stay:], slots, per).astype(jnp.bfloat16)
        lasts.append(pltpu.make_async_copy(packed_ref.at[k], out_refs[k], sems.at[2 + k]))
        lasts[-1].start()
    for last in lasts:
        last.wait()


def packed_rows(routes, hidden_in, copies, experts):
    tok_rows, width = hidden_in.shape
    stay = fold_of(tok_rows, width)[2]
    far = [pltpu.with_memory_space_constraint(x, pltpu.HBM) for x in (routes, hidden_in)]
    return pl.pallas_call(
        functools.partial(pack_kernel, copies, experts),
        out_shape=[jax.ShapeDtypeStruct((tok_rows, stay), jnp.bfloat16)] * experts,
        in_specs=[pl.BlockSpec(memory_space=pltpu.HBM)] * 2,
        out_specs=[pl.BlockSpec(memory_space=pl.ANY)] * experts,
        scratch_shapes=[
            pltpu.VMEM(routes.shape, jnp.int32),
            pltpu.VMEM(hidden_in.shape, jnp.bfloat16),
            pltpu.VMEM((experts, tok_rows, stay), jnp.bfloat16),
            pltpu.SemaphoreType.DMA((2 + experts,)),
        ],
        compiler_params=pltpu.CompilerParams(vmem_limit_bytes=8 * 1024 * 1024),
    )(*far)


def final_kernel(copies, experts, count, routes_far, hidden_far, *refs):
    far_refs, near_refs, refs = refs[: experts - 1], refs[experts - 1 : experts - 1 + count], refs[experts - 1 + count :]
    out_ref, routes_ref, hidden_ref, sems = refs
    moves = [(routes_far, routes_ref), (hidden_far, hidden_ref)]
    moves = [pltpu.make_async_copy(x, y, sems.at[k]) for k, (x, y) in enumerate(moves)]
    for move in moves:
        move.start()
    tok_rows, width = hidden_ref.shape
    slots, per, stay = fold_of(tok_rows, width)
    near = near_refs[0][...]
    for ref in near_refs[1:]:
        near = near + ref[...].astype(jnp.float32)
    parts = []
    for values in [near] + [ref[...].astype(jnp.float32) for ref in far_refs]:
        rest = unfolded(lambda at, size: values[:, at : at + size], tok_rows, width - stay, slots, per)
        parts.append(jnp.concatenate([values[:, :stay], rest], axis=1))
    own = lax.axis_index("expert") // copies
    moves[0].wait()
    _, column, _, rank, _, across = places(routes_ref, tok_rows)
    picks = []
    for k in range(experts):
        expert = jnp.bitwise_xor(own, k)
        picks.append(jnp.where((column == expert) & (rank == across) & (across < slots), 1.0, 0.0))
    pick = jnp.concatenate(picks, axis=1).astype(jnp.bfloat16)
    rows = jnp.concatenate(parts, axis=0).astype(jnp.bfloat16)
    routed = jnp.dot(pick, rows, preferred_element_type=jnp.float32)
    moves[1].wait()
    out_ref[...] = (hidden_ref[...].astype(jnp.float32) + routed).astype(jnp.bfloat16)


def placed_rows(routes, hidden_in, far_parts, near_parts, copies):
    experts = len(far_parts) + 1
    vmem = pl.BlockSpec(memory_space=pltpu.VMEM)
    return pl.pallas_call(
        functools.partial(final_kernel, copies, experts, len(near_parts)),
        out_shape=jax.ShapeDtypeStruct(hidden_in.shape, jnp.bfloat16),
        in_specs=[pl.BlockSpec(memory_space=pl.ANY)] * 2 + [vmem] * (len(far_parts) + len(near_parts)),
        out_specs=vmem,
        scratch_shapes=[
            pltpu.VMEM(routes.shape, jnp.int32),
            pltpu.VMEM(hidden_in.shape, jnp.bfloat16),
            pltpu.SemaphoreType.DMA((2,)),
        ],
        compiler_params=pltpu.CompilerParams(vmem_limit_bytes=8 * 1024 * 1024),
    )(routes, hidden_in, *far_parts, *near_parts)


def fetch_kernel(count, *refs):
    sources, targets, sems = refs[:count], refs[count + 1 : -1], refs[-1]
    moves = [pltpu.make_async_copy(a, b, sems.at[k]) for k, (a, b) in enumerate(zip(sources, targets))]
    for move in moves:
        move.start()
    for move in moves:
        move.wait()


def fetched(arrays, after):
    count = len(arrays)
    arrays = [pltpu.with_memory_space_constraint(x, pltpu.HBM) for x in arrays]
    size = sum(x.size * x.dtype.itemsize for x in arrays)
    return pl.pallas_call(
        functools.partial(fetch_kernel, count),
        out_shape=[jax.ShapeDtypeStruct(x.shape, x.dtype) for x in arrays],
        in_specs=[pl.BlockSpec(memory_space=pltpu.HBM)] * count + [pl.BlockSpec(memory_space=pl.ANY)],
        out_specs=[pl.BlockSpec(memory_space=pl.ANY)] * count,
        scratch_shapes=[pltpu.SemaphoreType.DMA((count,))],
        compiler_params=pltpu.CompilerParams(vmem_limit_bytes=1024 * 1024),
        cost_estimate=pl.CostEstimate(flops=0, bytes_accessed=size, transcendentals=0),
    )(*arrays, after)


def expert_kernel(copies, count, *refs):
    block_refs, refs = refs[:count], refs[count:]
    gain_ref, router_ref, up_ref, down_far = refs[:4]
    out_refs, (down_held, normed_ref, rest_ref, sems) = refs[4 : 4 + count], refs[4 + count :]
    tok_rows, width = block_refs[0].shape[0], down_far.shape[1]
    units = down_far.shape[0]
    slots, per, stay = fold_of(tok_rows, width)
    rest = width - stay
    parts = ((0, stay // 2), (stay // 2, stay // 2), (stay, rest)) if stay % 256 == 0 else ((0, stay), (stay, rest))
    piece = units
    waits = []
    for k in range(1):
        window = pl.ds(k * piece, piece)
        waits.append(pltpu.make_async_copy(down_far.at[window], down_held.at[window], sems.at[k]))
        waits[-1].start()
    pairs = [(first, block_refs[first : first + 2]) for first in range(0, count, 2)]

    def load(pair, at, size):
        return jnp.concatenate([ref[:, at : at + size].astype(jnp.float32) for ref in pair], axis=0)

    def unfold(ref):
        def window(at, size):
            return ref[:, at : at + size].astype(jnp.float32)

        return unfolded(window, tok_rows, rest, slots, per)

    factors = []
    for first, pair in pairs:
        values = jnp.concatenate([unfold(ref) for ref in pair], axis=0)
        rest_ref[first * tok_rows : (first + 2) * tok_rows, :] = values.astype(jnp.bfloat16)
        total = jnp.sum(values * values, axis=1, keepdims=True)
        for at, size in parts[:-1]:
            values = load(pair, at, size)
            total = total + jnp.sum(values * values, axis=1, keepdims=True)
        factors.append(lax.rsqrt(total * (1.0 / width) + 1e-06))
    nt = (((1,), (1,)), ((), ()))
    for at, size in parts:
        lines = [gain_ref[j : j + 1, :] for j in range(at // 128, (at + size) // 128)]
        gain = jnp.concatenate(lines, axis=1)
        for factor, (first, pair) in zip(factors, pairs):
            rows = slice(first * tok_rows, (first + 2) * tok_rows)
            values = load(pair, at, size) if at < stay else rest_ref[rows, :].astype(jnp.float32)
            normed_ref[rows, at : at + size] = (values * factor * gain).astype(jnp.bfloat16)
    logits = lax.dot_general(normed_ref[...], router_ref[...], nt, preferred_element_type=jnp.float32)
    lifted = lax.dot_general(normed_ref[...], up_ref[...], nt, preferred_element_type=jnp.float32)
    own = lax.axis_index("expert") // copies
    columns = lax.broadcasted_iota(jnp.int32, logits.shape, 1)
    logit = jnp.sum(jnp.where(columns == own, logits, 0.0), axis=1, keepdims=True)
    scores = 1.0 / (1.0 + jnp.exp(-logit))
    gate, up = lifted[:, :units], lifted[:, units:]
    act = (gate / (1.0 + jnp.exp(-gate)) * up).astype(jnp.bfloat16)
    for move in waits:
        move.wait()
    main = jnp.dot(act, down_held[:, :stay], preferred_element_type=jnp.float32) * scores
    ends = jnp.dot(act, down_held[:, stay:], preferred_element_type=jnp.float32) * scores
    for k in range(count):
        rows = slice(k * tok_rows, (k + 1) * tok_rows)
        out_refs[k][...] = folded(main[rows], ends[rows], slots, per).astype(jnp.bfloat16)


def expert_rows(blocks, norm_gain, router, gate_up, down_w, copies):
    count = len(blocks)
    tok_rows, width = blocks[0].shape[0], down_w.shape[1]
    units = down_w.shape[0]
    rows = count * tok_rows
    vmem = pl.BlockSpec(memory_space=pltpu.VMEM)
    return pl.pallas_call(
        functools.partial(expert_kernel, copies, count),
        out_shape=[jax.ShapeDtypeStruct(x.shape, jnp.bfloat16) for x in blocks],
        in_specs=[vmem] * (count + 3) + [pl.BlockSpec(memory_space=pltpu.HBM)],
        out_specs=[vmem] * count,
        scratch_shapes=[
            pltpu.VMEM(down_w.shape, jnp.bfloat16),
            pltpu.VMEM((rows, width), jnp.bfloat16),
            pltpu.VMEM((rows, width - blocks[0].shape[1]), jnp.bfloat16),
            pltpu.SemaphoreType.DMA((1,)),
        ],
        compiler_params=pltpu.CompilerParams(vmem_limit_bytes=32 * 1024 * 1024),
        cost_estimate=pl.CostEstimate(
            flops=6 * rows * width * units,
            bytes_accessed=6 * units * width,
            transcendentals=rows * units,
        ),
    )(*blocks, norm_gain, router, gate_up, pltpu.with_memory_space_constraint(down_w, pltpu.HBM))


def body(hidden_in, norm_gain, router, routes, routed_gate_up, routed_down):
    axis_len = lax.axis_size("expert")
    experts = router.shape[1]
    copies = axis_len // experts
    chips = list(range(2, copies, 2))[::-1]
    size = len(chips) + 1

    def swap(block, mask):
        return lax.ppermute(block, "expert", [(i, i ^ mask) for i in range(axis_len)])

    sources = list(packed_rows(routes.T, hidden_in, copies, experts))
    sources[1:] = [swap(sources[k], copies * k) for k in range(1, experts)]
    mine = [[source] + [swap(source, mask) for mask in chips] for source in sources]
    local = [routed_gate_up[0].T, router.T, norm_gain.reshape(-1, 128)]
    gate_up, router_t, gain = fetched(local, mine[0][-1])
    late = (mine[0][1:], [group[1:] for group in mine[1:]])
    gate_up, late = lax.optimization_barrier((gate_up, late))
    mine[0][1:] = late[0]
    for group, blocks in zip(mine[1:], late[1]):
        group[1:] = blocks
    theirs = [[swap(block, 1) for block in group] for group in mine]
    outs = expert_rows(sum(mine, []) + sum(theirs, []), gain, router_t, gate_up, routed_down[0], copies)
    kept = [outs[k * size : (k + 1) * size] for k in range(experts)]
    given = [outs[(experts + k) * size : (experts + k + 1) * size] for k in range(experts)]

    def both_cores(own_parts, given_parts):
        back = [swap(part, 1) for part in given_parts]
        both = [a.astype(jnp.float32) + b.astype(jnp.float32) for a, b in zip(own_parts, back)]
        return both[:1] + [part.astype(jnp.bfloat16) for part in both[1:]]

    def fold(both):
        total = both[0]
        for part, mask in zip(both[1:], chips):
            total = total + swap(part, mask).astype(jnp.float32)
        return total

    far_both = [both_cores(kept[k], given[k]) for k in range(1, experts)]
    firsts = [both[1] for both in far_both]
    firsts, given[0] = lax.optimization_barrier((firsts, given[0]))
    far_both = [both[:1] + [first] + both[2:] for both, first in zip(far_both, firsts)]
    sums = [fold(both).astype(jnp.bfloat16) for both in far_both]
    near = both_cores(kept[0], given[0])
    sums, near[3:] = lax.optimization_barrier((sums, near[3:]))
    near[1:] = [swap(part, mask) for part, mask in zip(near[1:], chips)]
    far_parts = [swap(total, copies * k) for k, total in enumerate(sums, start=1)]
    return placed_rows(routes.T, hidden_in, far_parts, near, copies)


def solution(mesh):
    placed = (
        P(("groups", "expert"), None),
        P(),
        P(),
        P(("groups", "expert"), None),
        P("expert", None, None),
        P("expert", None, None),
    )
    return jax.shard_map(
        body, mesh=mesh, in_specs=placed, out_specs=P(("groups", "expert"), None), check_vma=False
    )
```

```python
import functools

import jax
import jax.numpy as jnp
from jax import lax
from jax.experimental import pallas as pl
from jax.experimental.pallas import tpu as pltpu
from jax.sharding import PartitionSpec as P


def fold_of(tok_rows, width):
    slots = max(2, 3 * tok_rows // 4)
    per = -(-slots // (tok_rows - slots))
    rest = width // (per + 1) // 128 * 128
    return slots, per, width - rest


def folded(main, rest, slots, per):
    spare = []
    for first in range(0, slots, per):
        lines = [rest[k : k + 1] for k in range(first, min(first + per, slots))]
        pad = main.shape[1] - len(lines) * rest.shape[1]
        spare.append(jnp.concatenate(lines + [jnp.zeros((1, pad), jnp.float32)], axis=1))
    return jnp.concatenate([main[:slots]] + spare, axis=0)


def unfolded(load, tok_rows, rest, slots, per):
    lines = []
    for k in range(slots):
        at = k % per * rest
        lines.append(load(at, rest)[slots + k // per : slots + k // per + 1])
    return jnp.concatenate(lines + [jnp.zeros((tok_rows - slots, rest), jnp.float32)], axis=0)


def places(routes_ref, tok_rows):
    shape = (tok_rows, tok_rows)
    row = jnp.broadcast_to(routes_ref[...], shape)
    down = lax.broadcasted_iota(jnp.int32, shape, 0)
    across = lax.broadcasted_iota(jnp.int32, shape, 1)
    column = jnp.sum(jnp.where(down == across, row, 0), axis=1, keepdims=True)
    same = column == row
    rank_row = jnp.sum(jnp.where(same & (down < across), 1, 0), axis=0, keepdims=True)
    rank_column = jnp.sum(jnp.where(same & (across < down), 1, 0), axis=1, keepdims=True)
    return row, column, rank_row, rank_column, down, across


def pack_kernel(copies, experts, routes_far, hidden_far, *refs):
    out_refs, (routes_ref, hidden_ref, packed_ref, sems) = refs[:experts], refs[experts:]
    moves = [(routes_far, routes_ref), (hidden_far, hidden_ref)]
    moves = [pltpu.make_async_copy(x, y, sems.at[k]) for k, (x, y) in enumerate(moves)]
    for move in moves:
        move.start()
    tok_rows, width = hidden_ref.shape
    slots, per, stay = fold_of(tok_rows, width)
    own = lax.axis_index("expert") // copies
    moves[0].wait()
    row, _, rank, _, down, _ = places(routes_ref, tok_rows)
    picks = []
    for k in range(experts):
        expert = jnp.bitwise_xor(own, k)
        picks.append(jnp.where((row == expert) & (rank == down) & (down < slots), 1.0, 0.0))
    pick = jnp.concatenate(picks, axis=0).astype(jnp.bfloat16)
    moves[1].wait()
    sorted_rows = jnp.dot(pick, hidden_ref[...], preferred_element_type=jnp.float32)
    lasts = []
    for k in range(experts)[::-1]:
        rows = sorted_rows[k * tok_rows : (k + 1) * tok_rows]
        packed_ref[k] = folded(rows[:, :stay], rows[:, stay:], slots, per).astype(jnp.bfloat16)
        lasts.append(pltpu.make_async_copy(packed_ref.at[k], out_refs[k], sems.at[2 + k]))
        lasts[-1].start()
    for last in lasts:
        last.wait()


def packed_rows(routes, hidden_in, copies, experts):
    tok_rows, width = hidden_in.shape
    stay = fold_of(tok_rows, width)[2]
    far = [pltpu.with_memory_space_constraint(x, pltpu.HBM) for x in (routes, hidden_in)]
    return pl.pallas_call(
        functools.partial(pack_kernel, copies, experts),
        out_shape=[jax.ShapeDtypeStruct((tok_rows, stay), jnp.bfloat16)] * experts,
        in_specs=[pl.BlockSpec(memory_space=pltpu.HBM)] * 2,
        out_specs=[pl.BlockSpec(memory_space=pl.ANY)] * experts,
        scratch_shapes=[
            pltpu.VMEM(routes.shape, jnp.int32),
            pltpu.VMEM(hidden_in.shape, jnp.bfloat16),
            pltpu.VMEM((experts, tok_rows, stay), jnp.bfloat16),
            pltpu.SemaphoreType.DMA((2 + experts,)),
        ],
        compiler_params=pltpu.CompilerParams(vmem_limit_bytes=8 * 1024 * 1024),
    )(*far)


def final_kernel(copies, experts, count, routes_far, hidden_far, *refs):
    far_refs, near_refs, refs = refs[: experts - 1], refs[experts - 1 : experts - 1 + count], refs[experts - 1 + count :]
    out_ref, routes_ref, hidden_ref, sems = refs
    moves = [(routes_far, routes_ref), (hidden_far, hidden_ref)]
    moves = [pltpu.make_async_copy(x, y, sems.at[k]) for k, (x, y) in enumerate(moves)]
    for move in moves:
        move.start()
    tok_rows, width = hidden_ref.shape
    slots, per, stay = fold_of(tok_rows, width)
    near = near_refs[0][...]
    for ref in near_refs[1:]:
        near = near + ref[...].astype(jnp.float32)
    parts = []
    for values in [near] + [ref[...].astype(jnp.float32) for ref in far_refs]:
        rest = unfolded(lambda at, size: values[:, at : at + size], tok_rows, width - stay, slots, per)
        parts.append(jnp.concatenate([values[:, :stay], rest], axis=1))
    own = lax.axis_index("expert") // copies
    moves[0].wait()
    _, column, _, rank, _, across = places(routes_ref, tok_rows)
    picks = []
    for k in range(experts):
        expert = jnp.bitwise_xor(own, k)
        picks.append(jnp.where((column == expert) & (rank == across) & (across < slots), 1.0, 0.0))
    pick = jnp.concatenate(picks, axis=1).astype(jnp.bfloat16)
    rows = jnp.concatenate(parts, axis=0).astype(jnp.bfloat16)
    routed = jnp.dot(pick, rows, preferred_element_type=jnp.float32)
    moves[1].wait()
    out_ref[...] = (hidden_ref[...].astype(jnp.float32) + routed).astype(jnp.bfloat16)


def placed_rows(routes, hidden_in, far_parts, near_parts, copies):
    experts = len(far_parts) + 1
    vmem = pl.BlockSpec(memory_space=pltpu.VMEM)
    return pl.pallas_call(
        functools.partial(final_kernel, copies, experts, len(near_parts)),
        out_shape=jax.ShapeDtypeStruct(hidden_in.shape, jnp.bfloat16),
        in_specs=[pl.BlockSpec(memory_space=pl.ANY)] * 2 + [vmem] * (len(far_parts) + len(near_parts)),
        out_specs=vmem,
        scratch_shapes=[
            pltpu.VMEM(routes.shape, jnp.int32),
            pltpu.VMEM(hidden_in.shape, jnp.bfloat16),
            pltpu.SemaphoreType.DMA((2,)),
        ],
        compiler_params=pltpu.CompilerParams(vmem_limit_bytes=8 * 1024 * 1024),
    )(routes, hidden_in, *far_parts, *near_parts)


def fetch_kernel(count, size, *refs):
    sources, blocks, refs = refs[:count], refs[count : count + size], refs[count + size :]
    targets, joined, sems = refs[:count], refs[count], refs[count + 1]
    pairs = list(zip(sources, targets)) + [(block, joined.at[k]) for k, block in enumerate(blocks)]
    moves = [pltpu.make_async_copy(a, b, sems.at[k]) for k, (a, b) in enumerate(pairs)]
    for move in moves:
        move.start()
    for move in moves:
        move.wait()


def fetched(arrays, blocks):
    count, size = len(arrays), len(blocks)
    arrays = [pltpu.with_memory_space_constraint(x, pltpu.HBM) for x in arrays]
    total = sum(x.size * x.dtype.itemsize for x in arrays)
    joined = jax.ShapeDtypeStruct((size,) + blocks[0].shape, blocks[0].dtype)
    return pl.pallas_call(
        functools.partial(fetch_kernel, count, size),
        out_shape=[jax.ShapeDtypeStruct(x.shape, x.dtype) for x in arrays] + [joined],
        in_specs=[pl.BlockSpec(memory_space=pltpu.HBM)] * count + [pl.BlockSpec(memory_space=pl.ANY)] * size,
        out_specs=[pl.BlockSpec(memory_space=pl.ANY)] * (count + 1),
        scratch_shapes=[pltpu.SemaphoreType.DMA((count + size,))],
        compiler_params=pltpu.CompilerParams(vmem_limit_bytes=1024 * 1024),
        cost_estimate=pl.CostEstimate(flops=0, bytes_accessed=total, transcendentals=0),
    )(*arrays, *blocks)


def expert_kernel(copies, size, count, *refs):
    (mine_ref, theirs_ref), refs = refs[:2], refs[2:]
    mine_far, theirs_far, refs = refs[: count // 2 - size], refs[count // 2 - size : count - 2 * size], refs[count - 2 * size :]
    block_refs = [mine_ref.at[k] for k in range(size)] + list(mine_far)
    block_refs += [theirs_ref.at[k] for k in range(size)] + list(theirs_far)
    gain_ref, router_ref, up_ref, down_far = refs[:4]
    out_refs, (down_held, normed_ref, rest_ref, sems) = refs[4 : 4 + count], refs[4 + count :]
    tok_rows, width = block_refs[0].shape[0], down_far.shape[1]
    units = down_far.shape[0]
    slots, per, stay = fold_of(tok_rows, width)
    rest = width - stay
    parts = ((0, stay // 2), (stay // 2, stay // 2), (stay, rest)) if stay % 256 == 0 else ((0, stay), (stay, rest))
    piece = units
    waits = []
    for k in range(1):
        window = pl.ds(k * piece, piece)
        waits.append(pltpu.make_async_copy(down_far.at[window], down_held.at[window], sems.at[k]))
        waits[-1].start()
    pairs = [(first, block_refs[first : first + 2]) for first in range(0, count, 2)]

    def load(pair, at, size):
        return jnp.concatenate([ref[:, at : at + size].astype(jnp.float32) for ref in pair], axis=0)

    def unfold(ref):
        def window(at, size):
            return ref[:, at : at + size].astype(jnp.float32)

        return unfolded(window, tok_rows, rest, slots, per)

    factors = []
    for first, pair in pairs:
        values = jnp.concatenate([unfold(ref) for ref in pair], axis=0)
        rest_ref[first * tok_rows : (first + 2) * tok_rows, :] = values.astype(jnp.bfloat16)
        total = jnp.sum(values * values, axis=1, keepdims=True)
        for at, size in parts[:-1]:
            values = load(pair, at, size)
            total = total + jnp.sum(values * values, axis=1, keepdims=True)
        factors.append(lax.rsqrt(total * (1.0 / width) + 1e-06))
    nt = (((1,), (1,)), ((), ()))
    for at, size in parts:
        lines = [gain_ref[j : j + 1, :] for j in range(at // 128, (at + size) // 128)]
        gain = jnp.concatenate(lines, axis=1)
        for factor, (first, pair) in zip(factors, pairs):
            rows = slice(first * tok_rows, (first + 2) * tok_rows)
            values = load(pair, at, size) if at < stay else rest_ref[rows, :].astype(jnp.float32)
            normed_ref[rows, at : at + size] = (values * factor * gain).astype(jnp.bfloat16)
    logits = lax.dot_general(normed_ref[...], router_ref[...], nt, preferred_element_type=jnp.float32)
    lifted = lax.dot_general(normed_ref[...], up_ref[...], nt, preferred_element_type=jnp.float32)
    own = lax.axis_index("expert") // copies
    columns = lax.broadcasted_iota(jnp.int32, logits.shape, 1)
    logit = jnp.sum(jnp.where(columns == own, logits, 0.0), axis=1, keepdims=True)
    scores = 1.0 / (1.0 + jnp.exp(-logit))
    gate, up = lifted[:, :units], lifted[:, units:]
    act = (gate / (1.0 + jnp.exp(-gate)) * up).astype(jnp.bfloat16)
    for move in waits:
        move.wait()
    ends = jnp.dot(act, down_held[:, stay:], preferred_element_type=jnp.float32) * scores
    lines = {}
    for k in range(count):
        rest_rows = ends[k * tok_rows : (k + 1) * tok_rows]
        lines[k] = folded(jnp.zeros((tok_rows, stay), jnp.float32), rest_rows, slots, per)[slots:]
    for at, size_at in parts[:-1]:
        output = jnp.dot(act, down_held[:, at : at + size_at], preferred_element_type=jnp.float32) * scores
        for k in range(count):
            rows = [output[k * tok_rows : k * tok_rows + slots], lines[k][:, at : at + size_at]]
            out_refs[k][:, at : at + size_at] = jnp.concatenate(rows, axis=0).astype(jnp.bfloat16)


def expert_rows(own, blocks, norm_gain, router, gate_up, down_w, copies):
    size = own[0].shape[0]
    count = len(blocks) + 2 * size
    tok_rows, width = blocks[0].shape[0], down_w.shape[1]
    units = down_w.shape[0]
    rows = count * tok_rows
    vmem = pl.BlockSpec(memory_space=pltpu.VMEM)
    return pl.pallas_call(
        functools.partial(expert_kernel, copies, size, count),
        out_shape=[jax.ShapeDtypeStruct(blocks[0].shape, jnp.bfloat16)] * count,
        in_specs=[vmem] * (len(blocks) + 5) + [pl.BlockSpec(memory_space=pltpu.HBM)],
        out_specs=[vmem] * count,
        scratch_shapes=[
            pltpu.VMEM(down_w.shape, jnp.bfloat16),
            pltpu.VMEM((rows, width), jnp.bfloat16),
            pltpu.VMEM((rows, width - blocks[0].shape[1]), jnp.bfloat16),
            pltpu.SemaphoreType.DMA((1,)),
        ],
        compiler_params=pltpu.CompilerParams(vmem_limit_bytes=32 * 1024 * 1024),
        cost_estimate=pl.CostEstimate(
            flops=6 * rows * width * units,
            bytes_accessed=6 * units * width,
            transcendentals=rows * units,
        ),
    )(*own, *blocks, norm_gain, router, gate_up, pltpu.with_memory_space_constraint(down_w, pltpu.HBM))


def body(hidden_in, norm_gain, router, routes, routed_gate_up, routed_down):
    axis_len = lax.axis_size("expert")
    experts = router.shape[1]
    copies = axis_len // experts
    chips = list(range(2, copies, 2))[::-1]
    size = len(chips) + 1

    def swap(block, mask):
        return lax.ppermute(block, "expert", [(i, i ^ mask) for i in range(axis_len)])

    sources = list(packed_rows(routes.T, hidden_in, copies, experts))
    sources[1:] = [swap(sources[k], copies * k) for k in range(1, experts)]
    own_mine = [sources[0]] + [swap(sources[0], mask) for mask in chips]
    early = [swap(source, 1) for source in sources[1:]]
    late = [[swap(source, mask) for mask in chips] for source in sources[1:]]
    local = [routed_gate_up[0].T, router.T, norm_gain.reshape(-1, 128)]
    gate_up, router_t, gain, own = fetched(local, own_mine)
    gate_up, own, late = lax.optimization_barrier((gate_up, own, late))
    own = (own, swap(own, 1))
    mine = sum([[source] + group for source, group in zip(sources[1:], late)], [])
    theirs = sum([[first] + [swap(block, 1) for block in group] for first, group in zip(early, late)], [])
    outs = expert_rows(own, mine + theirs, gain, router_t, gate_up, routed_down[0], copies)
    kept = [outs[k * size : (k + 1) * size] for k in range(experts)]
    given = [outs[(experts + k) * size : (experts + k + 1) * size] for k in range(experts)]

    def both_cores(own_parts, given_parts):
        back = [swap(part, 1) for part in given_parts]
        both = [a.astype(jnp.float32) + b.astype(jnp.float32) for a, b in zip(own_parts, back)]
        return both[:1] + [part.astype(jnp.bfloat16) for part in both[1:]]

    def fold(both):
        total = both[0]
        for part, mask in zip(both[1:], chips):
            total = total + swap(part, mask).astype(jnp.float32)
        return total

    far_both = [both_cores(kept[k], given[k]) for k in range(1, experts)]
    firsts = [both[1] for both in far_both]
    firsts, given[0] = lax.optimization_barrier((firsts, given[0]))
    far_both = [both[:1] + [first] + both[2:] for both, first in zip(far_both, firsts)]
    sums = [fold(both).astype(jnp.bfloat16) for both in far_both]
    near = both_cores(kept[0], given[0])
    sums, near[3:] = lax.optimization_barrier((sums, near[3:]))
    near[1:] = [swap(part, mask) for part, mask in zip(near[1:], chips)]
    far_parts = [swap(total, copies * k) for k, total in enumerate(sums, start=1)]
    return placed_rows(routes.T, hidden_in, far_parts, near, copies)


def solution(mesh):
    placed = (
        P(("groups", "expert"), None),
        P(),
        P(),
        P(("groups", "expert"), None),
        P("expert", None, None),
        P("expert", None, None),
    )
    return jax.shard_map(
        body, mesh=mesh, in_specs=placed, out_specs=P(("groups", "expert"), None), check_vma=False
    )
```

```python
import functools

import jax
import jax.numpy as jnp
from jax import lax
from jax.experimental import pallas as pl
from jax.experimental.pallas import tpu as pltpu
from jax.sharding import PartitionSpec as P


def fold_of(tok_rows, width):
    slots = max(2, 3 * tok_rows // 4)
    per = -(-slots // (tok_rows - slots))
    rest = width // (per + 1) // 128 * 128
    return slots, per, width - rest


def folded(main, rest, slots, per):
    spare = []
    for first in range(0, slots, per):
        lines = [rest[k : k + 1] for k in range(first, min(first + per, slots))]
        pad = main.shape[1] - len(lines) * rest.shape[1]
        spare.append(jnp.concatenate(lines + [jnp.zeros((1, pad), jnp.float32)], axis=1))
    return jnp.concatenate([main[:slots]] + spare, axis=0)


def unfolded(load, tok_rows, rest, slots, per):
    lines = []
    for k in range(slots):
        at = k % per * rest
        lines.append(load(at, rest)[slots + k // per : slots + k // per + 1])
    return jnp.concatenate(lines + [jnp.zeros((tok_rows - slots, rest), jnp.float32)], axis=0)


def places(routes_ref, tok_rows):
    shape = (tok_rows, tok_rows)
    row = jnp.broadcast_to(routes_ref[...], shape)
    down = lax.broadcasted_iota(jnp.int32, shape, 0)
    across = lax.broadcasted_iota(jnp.int32, shape, 1)
    column = jnp.sum(jnp.where(down == across, row, 0), axis=1, keepdims=True)
    same = column == row
    rank_row = jnp.sum(jnp.where(same & (down < across), 1, 0), axis=0, keepdims=True)
    rank_column = jnp.sum(jnp.where(same & (across < down), 1, 0), axis=1, keepdims=True)
    return row, column, rank_row, rank_column, down, across


def pack_kernel(copies, experts, routes_far, hidden_far, *refs):
    out_refs, (routes_ref, hidden_ref, sems) = refs[:experts], refs[experts:]
    moves = [(routes_far, routes_ref), (hidden_far, hidden_ref)]
    moves = [pltpu.make_async_copy(x, y, sems.at[k]) for k, (x, y) in enumerate(moves)]
    for move in moves:
        move.start()
    tok_rows, width = hidden_ref.shape
    slots, per, stay = fold_of(tok_rows, width)
    own = lax.axis_index("expert") // copies
    moves[0].wait()
    row, _, rank, _, down, _ = places(routes_ref, tok_rows)
    picks = []
    for k in range(experts):
        expert = jnp.bitwise_xor(own, k)
        picks.append(jnp.where((row == expert) & (rank == down) & (down < slots), 1.0, 0.0))
    pick = jnp.concatenate(picks, axis=0).astype(jnp.bfloat16)
    moves[1].wait()
    sorted_rows = jnp.dot(pick, hidden_ref[...], preferred_element_type=jnp.float32)
    for k in range(experts):
        rows = sorted_rows[k * tok_rows : (k + 1) * tok_rows]
        out_refs[k][...] = folded(rows[:, :stay], rows[:, stay:], slots, per).astype(jnp.bfloat16)


def packed_rows(routes, hidden_in, copies, experts):
    tok_rows, width = hidden_in.shape
    stay = fold_of(tok_rows, width)[2]
    far = [pltpu.with_memory_space_constraint(x, pltpu.HBM) for x in (routes, hidden_in)]
    return pl.pallas_call(
        functools.partial(pack_kernel, copies, experts),
        out_shape=[jax.ShapeDtypeStruct((tok_rows, stay), jnp.bfloat16)] * experts,
        in_specs=[pl.BlockSpec(memory_space=pltpu.HBM)] * 2,
        out_specs=[pl.BlockSpec(memory_space=pltpu.VMEM)] * experts,
        scratch_shapes=[
            pltpu.VMEM(routes.shape, jnp.int32),
            pltpu.VMEM(hidden_in.shape, jnp.bfloat16),
            pltpu.SemaphoreType.DMA((2,)),
        ],
        compiler_params=pltpu.CompilerParams(vmem_limit_bytes=8 * 1024 * 1024),
    )(*far)


def final_kernel(copies, experts, count, routes_far, hidden_far, *refs):
    far_refs, near_refs, refs = refs[: experts - 1], refs[experts - 1 : experts - 1 + count], refs[experts - 1 + count :]
    out_ref, routes_ref, hidden_ref, sems = refs
    moves = [(routes_far, routes_ref), (hidden_far, hidden_ref)]
    moves = [pltpu.make_async_copy(x, y, sems.at[k]) for k, (x, y) in enumerate(moves)]
    for move in moves:
        move.start()
    tok_rows, width = hidden_ref.shape
    slots, per, stay = fold_of(tok_rows, width)
    near = near_refs[0][...]
    for ref in near_refs[1:]:
        near = near + ref[...].astype(jnp.float32)
    parts = []
    for values in [near] + [ref[...].astype(jnp.float32) for ref in far_refs]:
        rest = unfolded(lambda at, size: values[:, at : at + size], tok_rows, width - stay, slots, per)
        parts.append(jnp.concatenate([values[:, :stay], rest], axis=1))
    own = lax.axis_index("expert") // copies
    moves[0].wait()
    _, column, _, rank, _, across = places(routes_ref, tok_rows)
    picks = []
    for k in range(experts):
        expert = jnp.bitwise_xor(own, k)
        picks.append(jnp.where((column == expert) & (rank == across) & (across < slots), 1.0, 0.0))
    pick = jnp.concatenate(picks, axis=1).astype(jnp.bfloat16)
    rows = jnp.concatenate(parts, axis=0).astype(jnp.bfloat16)
    routed = jnp.dot(pick, rows, preferred_element_type=jnp.float32)
    moves[1].wait()
    out_ref[...] = (hidden_ref[...].astype(jnp.float32) + routed).astype(jnp.bfloat16)


def placed_rows(routes, hidden_in, far_parts, near_parts, copies):
    experts = len(far_parts) + 1
    vmem = pl.BlockSpec(memory_space=pltpu.VMEM)
    return pl.pallas_call(
        functools.partial(final_kernel, copies, experts, len(near_parts)),
        out_shape=jax.ShapeDtypeStruct(hidden_in.shape, jnp.bfloat16),
        in_specs=[pl.BlockSpec(memory_space=pl.ANY)] * 2 + [vmem] * (len(far_parts) + len(near_parts)),
        out_specs=vmem,
        scratch_shapes=[
            pltpu.VMEM(routes.shape, jnp.int32),
            pltpu.VMEM(hidden_in.shape, jnp.bfloat16),
            pltpu.SemaphoreType.DMA((2,)),
        ],
        compiler_params=pltpu.CompilerParams(vmem_limit_bytes=8 * 1024 * 1024),
    )(routes, hidden_in, *far_parts, *near_parts)


def fetch_kernel(count, size, *refs):
    sources, blocks, refs = refs[:count], refs[count : count + size], refs[count + size :]
    targets, joined, sems = refs[:count], refs[count], refs[count + 1]
    pairs = list(zip(sources, targets)) + [(block, joined.at[k]) for k, block in enumerate(blocks)]
    moves = [pltpu.make_async_copy(a, b, sems.at[k]) for k, (a, b) in enumerate(pairs)]
    for move in moves:
        move.start()
    for move in moves:
        move.wait()


def fetched(arrays, blocks):
    count, size = len(arrays), len(blocks)
    arrays = [pltpu.with_memory_space_constraint(x, pltpu.HBM) for x in arrays]
    total = sum(x.size * x.dtype.itemsize for x in arrays)
    joined = jax.ShapeDtypeStruct((size,) + blocks[0].shape, blocks[0].dtype)
    return pl.pallas_call(
        functools.partial(fetch_kernel, count, size),
        out_shape=[jax.ShapeDtypeStruct(x.shape, x.dtype) for x in arrays] + [joined],
        in_specs=[pl.BlockSpec(memory_space=pltpu.HBM)] * count + [pl.BlockSpec(memory_space=pl.ANY)] * size,
        out_specs=[pl.BlockSpec(memory_space=pl.ANY)] * (count + 1),
        scratch_shapes=[pltpu.SemaphoreType.DMA((count + size,))],
        compiler_params=pltpu.CompilerParams(vmem_limit_bytes=1024 * 1024),
        cost_estimate=pl.CostEstimate(flops=0, bytes_accessed=total, transcendentals=0),
    )(*arrays, *blocks)


def expert_kernel(copies, size, count, *refs):
    (mine_ref, theirs_ref), refs = refs[:2], refs[2:]
    mine_far, theirs_far, refs = refs[: count // 2 - size], refs[count // 2 - size : count - 2 * size], refs[count - 2 * size :]
    block_refs = [mine_ref.at[k] for k in range(size)] + list(mine_far)
    block_refs += [theirs_ref.at[k] for k in range(size)] + list(theirs_far)
    gain_ref, router_ref, up_ref, down_far = refs[:4]
    out_refs, (down_held, normed_ref, rest_ref, sems) = refs[4 : 4 + count], refs[4 + count :]
    tok_rows, width = block_refs[0].shape[0], down_far.shape[1]
    units = down_far.shape[0]
    slots, per, stay = fold_of(tok_rows, width)
    rest = width - stay
    parts = ((0, stay // 2), (stay // 2, stay // 2), (stay, rest)) if stay % 256 == 0 else ((0, stay), (stay, rest))
    piece = units
    waits = []
    for k in range(1):
        window = pl.ds(k * piece, piece)
        waits.append(pltpu.make_async_copy(down_far.at[window], down_held.at[window], sems.at[k]))
        waits[-1].start()
    pairs = [(first, block_refs[first : first + 2]) for first in range(0, count, 2)]

    def load(pair, at, size):
        return jnp.concatenate([ref[:, at : at + size].astype(jnp.float32) for ref in pair], axis=0)

    def unfold(ref):
        def window(at, size):
            return ref[:, at : at + size].astype(jnp.float32)

        return unfolded(window, tok_rows, rest, slots, per)

    factors = []
    for first, pair in pairs:
        values = jnp.concatenate([unfold(ref) for ref in pair], axis=0)
        rest_ref[first * tok_rows : (first + 2) * tok_rows, :] = values.astype(jnp.bfloat16)
        total = jnp.sum(values * values, axis=1, keepdims=True)
        for at, size in parts[:-1]:
            values = load(pair, at, size)
            total = total + jnp.sum(values * values, axis=1, keepdims=True)
        factors.append(lax.rsqrt(total * (1.0 / width) + 1e-06))
    nt = (((1,), (1,)), ((), ()))
    for at, size in parts:
        lines = [gain_ref[j : j + 1, :] for j in range(at // 128, (at + size) // 128)]
        gain = jnp.concatenate(lines, axis=1)
        for factor, (first, pair) in zip(factors, pairs):
            rows = slice(first * tok_rows, (first + 2) * tok_rows)
            values = load(pair, at, size) if at < stay else rest_ref[rows, :].astype(jnp.float32)
            normed_ref[rows, at : at + size] = (values * factor * gain).astype(jnp.bfloat16)
    logits = lax.dot_general(normed_ref[...], router_ref[...], nt, preferred_element_type=jnp.float32)
    lifted = lax.dot_general(normed_ref[...], up_ref[...], nt, preferred_element_type=jnp.float32)
    own = lax.axis_index("expert") // copies
    columns = lax.broadcasted_iota(jnp.int32, logits.shape, 1)
    logit = jnp.sum(jnp.where(columns == own, logits, 0.0), axis=1, keepdims=True)
    scores = 1.0 / (1.0 + jnp.exp(-logit))
    gate, up = lifted[:, :units], lifted[:, units:]
    act = (gate / (1.0 + jnp.exp(-gate)) * up * scores).astype(jnp.bfloat16)
    for move in waits:
        move.wait()
    ends = jnp.dot(act, down_held[:, stay:], preferred_element_type=jnp.float32)
    lines = {}
    for k in range(count):
        rest_rows = ends[k * tok_rows : (k + 1) * tok_rows]
        lines[k] = folded(jnp.zeros((tok_rows, stay), jnp.float32), rest_rows, slots, per)[slots:]
    for at, size_at in parts[:-1]:
        output = jnp.dot(act, down_held[:, at : at + size_at], preferred_element_type=jnp.float32)
        for k in range(count):
            rows = [output[k * tok_rows : k * tok_rows + slots], lines[k][:, at : at + size_at]]
            out_refs[k][:, at : at + size_at] = jnp.concatenate(rows, axis=0).astype(jnp.bfloat16)


def expert_rows(own, blocks, norm_gain, router, gate_up, down_w, copies):
    size = own[0].shape[0]
    count = len(blocks) + 2 * size
    tok_rows, width = blocks[0].shape[0], down_w.shape[1]
    units = down_w.shape[0]
    rows = count * tok_rows
    vmem = pl.BlockSpec(memory_space=pltpu.VMEM)
    return pl.pallas_call(
        functools.partial(expert_kernel, copies, size, count),
        out_shape=[jax.ShapeDtypeStruct(blocks[0].shape, jnp.bfloat16)] * count,
        in_specs=[vmem] * (len(blocks) + 5) + [pl.BlockSpec(memory_space=pltpu.HBM)],
        out_specs=[vmem] * count,
        scratch_shapes=[
            pltpu.VMEM(down_w.shape, jnp.bfloat16),
            pltpu.VMEM((rows, width), jnp.bfloat16),
            pltpu.VMEM((rows, width - blocks[0].shape[1]), jnp.bfloat16),
            pltpu.SemaphoreType.DMA((1,)),
        ],
        compiler_params=pltpu.CompilerParams(vmem_limit_bytes=32 * 1024 * 1024),
        cost_estimate=pl.CostEstimate(
            flops=6 * rows * width * units,
            bytes_accessed=6 * units * width,
            transcendentals=rows * units,
        ),
    )(*own, *blocks, norm_gain, router, gate_up, pltpu.with_memory_space_constraint(down_w, pltpu.HBM))


def body(hidden_in, norm_gain, router, routes, routed_gate_up, routed_down):
    axis_len = lax.axis_size("expert")
    experts = router.shape[1]
    copies = axis_len // experts
    chips = list(range(2, copies, 2))[::-1]
    size = len(chips) + 1

    def swap(block, mask):
        return lax.ppermute(block, "expert", [(i, i ^ mask) for i in range(axis_len)])

    sources = list(packed_rows(routes.T, hidden_in, copies, experts))
    sources[1:] = [swap(sources[k], copies * k) for k in range(1, experts)]
    own_mine = [sources[0]] + [swap(sources[0], mask) for mask in chips]
    early = [swap(source, 1) for source in sources[1:]]
    late = [[swap(source, mask) for mask in chips] for source in sources[1:]]
    local = [routed_gate_up[0].T, router.T, norm_gain.reshape(-1, 128)]
    gate_up, router_t, gain, own = fetched(local, own_mine)
    gate_up, own, late = lax.optimization_barrier((gate_up, own, late))
    own = (own, swap(own, 1))
    mine = sum([[source] + group for source, group in zip(sources[1:], late)], [])
    theirs = sum([[first] + [swap(block, 1) for block in group] for first, group in zip(early, late)], [])
    outs = expert_rows(own, mine + theirs, gain, router_t, gate_up, routed_down[0], copies)
    kept = [outs[k * size : (k + 1) * size] for k in range(experts)]
    given = [outs[(experts + k) * size : (experts + k + 1) * size] for k in range(experts)]

    def both_cores(own_parts, given_parts):
        back = [swap(part, 1) for part in given_parts]
        both = [a.astype(jnp.float32) + b.astype(jnp.float32) for a, b in zip(own_parts, back)]
        return both[:1] + [part.astype(jnp.bfloat16) for part in both[1:]]

    def fold(both):
        total = both[0]
        for part, mask in zip(both[1:], chips):
            total = total + swap(part, mask).astype(jnp.float32)
        return total

    far_both = [both_cores(kept[k], given[k]) for k in range(1, experts)]
    firsts = [both[1] for both in far_both]
    firsts, given[0] = lax.optimization_barrier((firsts, given[0]))
    far_both = [both[:1] + [first] + both[2:] for both, first in zip(far_both, firsts)]
    sums = [fold(both).astype(jnp.bfloat16) for both in far_both]
    near = both_cores(kept[0], given[0])
    sums, near[3:] = lax.optimization_barrier((sums, near[3:]))
    near[1:] = [swap(part, mask) for part, mask in zip(near[1:], chips)]
    far_parts = [swap(total, copies * k) for k, total in enumerate(sums, start=1)]
    return placed_rows(routes.T, hidden_in, far_parts, near, copies)


def solution(mesh):
    placed = (
        P(("groups", "expert"), None),
        P(),
        P(),
        P(("groups", "expert"), None),
        P("expert", None, None),
        P("expert", None, None),
    )
    return jax.shard_map(
        body, mesh=mesh, in_specs=placed, out_specs=P(("groups", "expert"), None), check_vma=False
    )
```
